32 devices in a mesh: gz: 8 (over y, x, core), gy: 4 (over z).
Axes of the slice: x: 2, y: 2, z: 4, core: 2. Of those that a mesh axis runs over, the one named last changes fastest.
Arguments:
- electric: float32 [3, 128, 32, 256], P(None, 'gz', 'gy'), may hold values from -6 to 6
- magnetic: float32 [3, 128, 32, 256], P(None, 'gz', 'gy'), may hold values from -6 to 6
- material: int32 [128, 32, 256], P('gz', 'gy'), may hold values from 0 to 15
- incoming: int32 [32, 32, 256], P(None, 'gy'), may hold values from 0 to 15
- shift_flags: int32 [8], replicated, may hold values from 0 to 1, as said below
- eps_table: float32 [16], replicated, may hold values from 1 to 6
- sigma_table: float32 [16], replicated, may hold values from 0 to 1
- kerr_table: float32 [16], replicated, may hold values from 0.05 to 0.5
Outputs:
- electric_out: float32 [3, 128, 32, 256], P(None, 'gz', 'gy')
- magnetic_out: float32 [3, 128, 32, 256], P(None, 'gz', 'gy')
The draws below stay inside these ranges and needn't reach their ends.
Inputs may be any that keep to these rules, and one draw needn't show every extreme that they name: `shift_flags`: exactly 4 entries are 1, the others 0.
All inputs are finite; a program needn't handle non-finite values.
Results may differ from the reference program's by a relative error of at most 0.00002.
Values sent between devices are 32-bit elements; how exact they have to be, the bound alone decides.
No kernel may reach another device: no remote copies, remote signals or barrier semaphores. Data moves between devices by JAX's collectives and lax.ppermute only.
A program may use at most 64 MiB of HBM per device.

```python
import math
import jax
import jax.numpy as jnp
from jax import lax

NX = 256
STEPS = 8
SHIFTS = 4
SHIFT = 8
MAT = 16
NZ = 128
NY = 32


def draw_shift_flags(key, part):
    ranking = jax.random.permutation(key, STEPS)
    return (ranking < SHIFTS).astype(jnp.int32)


def set_ends(drawn, key, smallest, top_value):
    dims = drawn.shape
    place = [jax.random.randint(jax.random.fold_in(key, axis), (), 0, dims[axis]) for axis in range(len(dims))]
    drawn = drawn.at[tuple(place)].set(smallest)
    longest = dims.index(max(dims))
    place[longest] = (place[longest] + 1) % dims[longest]
    return drawn.at[tuple(place)].set(top_value)


def levels(stream_key, extent, pieces, smallest, top_value):
    level = 1.0
    for position, blocks in pieces:
        heights = jax.random.uniform(jax.random.fold_in(jax.random.fold_in(stream_key, 6), position), (blocks,), jnp.float32, smallest / len(pieces), top_value / len(pieces))
        level = level * jnp.repeat(jnp.exp(heights), extent[position] // blocks).reshape((-1,) + (1,) * (len(extent) - 1 - position))
    return level


def gaussian(stream_key, shape, deviation, most, split=(), held_as=jnp.bfloat16):
    result = jax.random.normal(stream_key, shape, jnp.float32) * deviation
    if len(split) > 0:
        result = levels(stream_key, shape, split, -0.22, 0.18) * result
    return jnp.clip(result, min=-most, max=most).astype(held_as)


def setup_inputs(seed: int = 0) -> dict:
    streams_of = jax.random.split(jax.random.key(seed), 9)
    electric = gaussian(streams_of[0], (3, NZ, NY, NX), 1.0, 6.0, ((1, 8), (2, 4)), jnp.float32)
    magnetic = gaussian(streams_of[1], (3, NZ, NY, NX), 1.0, 6.0, ((1, 8), (2, 4)), jnp.float32)
    material = set_ends(jax.random.randint(streams_of[2], (NZ, NY, NX), 0, MAT), jax.random.fold_in(streams_of[2], 1), 0, MAT - 1).astype(jnp.int32)
    incoming = set_ends(jax.random.randint(streams_of[3], (SHIFTS * SHIFT, NY, NX), 0, MAT), jax.random.fold_in(streams_of[3], 1), 0, MAT - 1).astype(jnp.int32)
    shift_flags = draw_shift_flags(jax.random.fold_in(streams_of[8], 71), 0)
    eps_table = jnp.clip(jnp.exp(jax.random.uniform(streams_of[5], (MAT,), jnp.float32, math.log(1.0), math.log(6.0))), 1.0, 6.0)
    sigma_table = jnp.clip(jax.random.uniform(streams_of[6], (MAT,), jnp.float32, 0.0, 1.0), 0.0, 1.0)
    kerr_table = jnp.clip(jax.random.uniform(streams_of[7], (MAT,), jnp.float32, 0.05, 0.5), 0.05, 0.5)
    return {"electric": electric, "magnetic": magnetic, "material": material, "incoming": incoming, "shift_flags": shift_flags, "eps_table": eps_table, "sigma_table": sigma_table, "kerr_table": kerr_table}


courant_number = 0.5


def forward_diff(field, axis_no):
    length = field.shape[axis_no]
    shifted = jnp.concatenate([lax.slice_in_dim(field, 1, length, axis=axis_no), jnp.zeros_like(lax.slice_in_dim(field, 0, 1, axis=axis_no))], axis=axis_no)
    return shifted - field


def backward_diff(field, axis_no):
    length = field.shape[axis_no]
    shifted = jnp.concatenate([jnp.zeros_like(lax.slice_in_dim(field, 0, 1, axis=axis_no)), lax.slice_in_dim(field, 0, length - 1, axis=axis_no)], axis=axis_no)
    return field - shifted


def curl_parts(vector, differ):
    part_x = differ(vector[2], 1) - differ(vector[1], 0)
    part_y = differ(vector[0], 0) - differ(vector[2], 2)
    part_z = differ(vector[1], 2) - differ(vector[0], 1)
    return jnp.stack([part_x, part_y, part_z])


def e_update(electric, curl_h, coefs):
    square = electric[0] * electric[0] + electric[1] * electric[1] + electric[2] * electric[2]
    permit = coefs[0] + coefs[2] * square
    damping = 0.5 * coefs[1] / permit
    return ((1.0 - damping) * electric + (courant_number / permit) * curl_h) / (1.0 + damping)


def lookup(id_map, eps_table, sigma_table, kerr_table):
    return jnp.stack([eps_table[id_map], sigma_table[id_map], kerr_table[id_map]])


def reference(electric, magnetic, material, incoming, shift_flags, eps_table, sigma_table, kerr_table):
    coefs = lookup(material, eps_table, sigma_table, kerr_table)
    done_count = jnp.int32(0)
    for step_no in range(STEPS):
        shift_on = shift_flags[step_no] == 1
        new_ids = lax.dynamic_slice_in_dim(incoming, (done_count * SHIFT).astype(jnp.int32), SHIFT, 0)
        new_coefs = lookup(new_ids, eps_table, sigma_table, kerr_table)
        zero_planes = jnp.zeros((3, SHIFT, NY, NX), jnp.float32)
        electric = jnp.where(shift_on, jnp.concatenate([electric[:, SHIFT:], zero_planes], 1), electric)
        magnetic = jnp.where(shift_on, jnp.concatenate([magnetic[:, SHIFT:], zero_planes], 1), magnetic)
        coefs = jnp.where(shift_on, jnp.concatenate([coefs[:, SHIFT:], new_coefs], 1), coefs)
        done_count = done_count + shift_flags[step_no]
        magnetic = magnetic - courant_number * curl_parts(electric, forward_diff)
        electric = e_update(electric, curl_parts(magnetic, backward_diff), coefs)
    return electric, magnetic
```

```python
import functools

import jax
import jax.numpy as jnp
from jax import lax
from jax.experimental import pallas as pl
from jax.experimental.pallas import tpu as pltpu
from jax.sharding import PartitionSpec as P

STEPS = 8
SHIFTS = 4
SHIFT = 8
HALO = STEPS
MAT = 16
LANES = 128


def permute(value, axis, pairs):
    return lax.ppermute(value, axis, pairs)


def neighbour(value, axis, hop):
    count = lax.axis_size(axis)
    pairs = [(s, s + hop) for s in range(count) if 0 <= s + hop < count]
    return permute(value, axis, pairs)


def swap_cores(value):
    return permute(value, "gz", [(s, s ^ 1) for s in range(lax.axis_size("gz"))])


def outer_halo(value):
    count = lax.axis_size("gz")
    pairs = [(s, s - 1) for s in range(1, count, 2)]
    pairs += [(s, s - 3) for s in range(4, count, 2)]
    pairs += [(0, count - 3)]
    return permute(value, "gz", pairs)


def step_kernel(
    planes, rows,
    pos, flags, tables,
    e_dn, e_mid, e_up, h_dn, h_mid, h_up,
    ze_dn, ze_mid, ze_up, zh_dn, zh_mid, zh_up,
    o_dn, o_mid, o_up,
    e_out, h_out,
    E, H, M, A, B, K, sems, out_sems,
):
    gz, gy, last_y = pos[0], pos[1], pos[2]
    top_z = pos[3]
    wide = planes + 2 * HALO
    odd = lax.rem(gz, 2)
    inner_at = pl.multiple_of((1 - odd) * (planes + HALO), HALO)
    outer_at = pl.multiple_of(odd * (planes + HALO), HALO)
    copies = []

    def copy(src, dst):
        one = pltpu.make_async_copy(src, dst, sems.at[len(copies)])
        one.start()
        copies.append(one)

    for b, (e, h, ze, zh, o) in enumerate(
        ((e_dn, h_dn, ze_dn, zh_dn, o_dn), (e_mid, h_mid, ze_mid, zh_mid, o_mid), (e_up, h_up, ze_up, zh_up, o_up))
    ):
        at = pl.ds(b * rows, rows)
        main, inner, outer = pl.ds(HALO, planes), pl.ds(inner_at, HALO), pl.ds(outer_at, HALO)
        copy(h.at[3], M.at[main, at])
        copy(zh.at[3], M.at[inner, at])
        copy(o.at[6], M.at[outer, at])
        copy(e, E.at[:, main, at])
        copy(ze, E.at[:, inner, at])
        copy(o.at[pl.ds(0, 3)], E.at[:, outer, at])
        copy(h.at[pl.ds(0, 3)], H.at[:, main, at])
        copy(zh.at[pl.ds(0, 3)], H.at[:, inner, at])
        copy(o.at[pl.ds(3, 3)], H.at[:, outer, at])
    for one in copies:
        one.wait()

    tile = (8, LANES)
    lane = lax.broadcasted_iota(jnp.int32, tile, 1)
    sub = lax.broadcasted_iota(jnp.int32, tile, 0)
    lane_first, lane_last = lane == 0, lane == LANES - 1
    sub_first, sub_last = sub == 0, sub == 7
    zero = jnp.zeros(tile, jnp.float32)
    tiles = 3
    below = jnp.where(gy == 0, 0.0, 1.0).astype(jnp.float32)
    above = jnp.where(gy == last_y, 0.0, 1.0).astype(jnp.float32)
    halves = (slice(0, LANES), slice(LANES, 2 * LANES))

    def spot(t):
        return slice(8 * t, 8 * t + 8)

    tab = [tables[i] for i in range(3)]

    def prepare(p, carry):
        for t in range(tiles):
            for x in halves:
                ids = M[p, spot(t), x].astype(jnp.int32)
                for out, table in zip((A, B, K), tab):
                    out[p, spot(t), x] = jnp.take_along_axis(table, ids, axis=1)
                for c in range(3):
                    H[c, p, spot(t), x] = 2.0 * H[c, p, spot(t), x]
        return carry

    lax.fori_loop(0, wide, prepare, 0)
    E[:, wide] = jnp.zeros((3, tiles * 8, 2 * LANES), jnp.float32)

    def load(ref, c, p, t):
        return [ref[c, p, spot(t), x] for x in halves]

    def x_next(v):
        r = [pltpu.roll(a, LANES - 1, 1) for a in v]
        return [jnp.where(lane_last, r[1], r[0]), jnp.where(lane_last, zero, r[1])]

    def x_prev(v):
        r = [pltpu.roll(a, 1, 1) for a in v]
        return [jnp.where(lane_first, zero, r[0]), jnp.where(lane_first, r[0], r[1])]

    def y_next(parts):
        r = [[pltpu.roll(a, 7, 0) for a in v] for v in parts]
        result = []
        for t in range(tiles):
            if t == tiles - 1:
                result.append(r[t])
                continue
            far = r[t + 1] if t != 1 else [a * above for a in r[t + 1]]
            result.append([jnp.where(sub_last, a, b) for a, b in zip(far, r[t])])
        return result

    def y_prev(parts):
        r = [[pltpu.roll(a, 1, 0) for a in v] for v in parts]
        result = []
        for t in range(tiles):
            if t == 0:
                result.append(r[t])
                continue
            far = r[t - 1] if t != 1 else [a * below for a in r[t - 1]]
            result.append([jnp.where(sub_first, a, b) for a, b in zip(far, r[t])])
        return result

    def magnetic_plane(p):
        ex, ey, ez = [[load(E, c, p, t) for t in range(tiles)] for c in range(3)]
        ez_y, ex_y = y_next(ez), y_next(ex)
        for t in range(tiles):
            ez_x, ey_x = x_next(ez[t]), x_next(ey[t])
            ey_z, ex_z = load(E, 1, p + 1, t), load(E, 0, p + 1, t)
            hx, hy, hz = [load(H, c, p, t) for c in range(3)]
            for i, x in enumerate(halves):
                H[0, p, spot(t), x] = hx[i] - ((ez_y[t][i] - ez[t][i]) - (ey_z[i] - ey[t][i]))
                H[1, p, spot(t), x] = hy[i] - ((ex_z[i] - ex[t][i]) - (ez_x[i] - ez[t][i]))
                H[2, p, spot(t), x] = hz[i] - ((ey_x[i] - ey[t][i]) - (ex_y[t][i] - ex[t][i]))

    def electric_plane(p):
        hx, hy, hz = [[load(H, c, p, t) for t in range(tiles)] for c in range(3)]
        hz_y, hx_y = y_prev(hz), y_prev(hx)
        for t in range(tiles):
            hz_x, hy_x = x_prev(hz[t]), x_prev(hy[t])
            hy_z, hx_z = load(H, 1, p - 1, t), load(H, 0, p - 1, t)
            ex, ey, ez = [load(E, c, p, t) for c in range(3)]
            for i, x in enumerate(halves):
                cx = (hz[t][i] - hz_y[t][i]) - (hy[t][i] - hy_z[i])
                cy = (hx[t][i] - hx_z[i]) - (hz[t][i] - hz_x[i])
                cz = (hy[t][i] - hy_x[i]) - (hx[t][i] - hx_y[t][i])
                n = K[p, spot(t), x] * (ex[i] * ex[i] + ey[i] * ey[i] + ez[i] * ez[i])
                up = A[p, spot(t), x] + n
                down = B[p, spot(t), x] + n
                guess = pl.reciprocal(down, approx=True)
                r = guess * (2.0 - down * guess)
                E[0, p, spot(t), x] = (up * ex[i] + cx) * r
                E[1, p, spot(t), x] = (up * ey[i] + cy) * r
                E[2, p, spot(t), x] = (up * ez[i] + cz) * r

    def zero_plane(ref, p):
        @pl.when((p >= 0) & (p < wide))
        def _():
            ref[:, p] = jnp.zeros((3, tiles * 8, 2 * LANES), jnp.float32)

    base = planes * gz + SHIFT * SHIFTS - HALO

    def step(s, moved):
        moved = moved + flags[s - 1]

        def magnetic_loop(p, carry):
            magnetic_plane(p)
            return carry

        def electric_loop(p, carry):
            electric_plane(p)
            return carry

        lax.fori_loop(s - 1, wide - s, magnetic_loop, 0)
        zero_plane(H, SHIFT * moved - 1 - base)
        lax.fori_loop(s, wide - s, electric_loop, 0)
        zero_plane(E, top_z + SHIFT * moved - base)
        return moved

    lax.fori_loop(1, STEPS + 1, step, jnp.int32(0))

    def finish(p, carry):
        for c in range(3):
            for x in halves:
                H[c, p, spot(1), x] = 0.5 * H[c, p, spot(1), x]
        return carry

    lax.fori_loop(HALO, HALO + planes, finish, 0)
    outs = [
        pltpu.make_async_copy(ref.at[:, pl.ds(HALO, planes), pl.ds(rows, rows)], out, out_sems.at[i])
        for i, (ref, out) in enumerate(((E, e_out), (H, h_out)))
    ]
    for one in outs:
        one.start()
    for one in outs:
        one.wait()


def run_steps(pos, flags, tables, pieces, planes, rows, width):
    wide = planes + 2 * HALO
    tall = 3 * rows
    smem = pl.BlockSpec(memory_space=pltpu.SMEM)
    field = jax.ShapeDtypeStruct((3, planes, rows, width), jnp.float32)
    vec = [(3, wide + 1, tall, width), (3, wide, tall, width)] + [(wide, tall, width)] * 4
    return pl.pallas_call(
        functools.partial(step_kernel, planes, rows),
        out_shape=(field, field),
        in_specs=[smem, smem, pl.BlockSpec(memory_space=pltpu.VMEM)] + [pl.BlockSpec(memory_space=pl.ANY)] * len(pieces),
        out_specs=(pl.BlockSpec(memory_space=pl.ANY),) * 2,
        scratch_shapes=[pltpu.VMEM(shape, jnp.float32) for shape in vec]
        + [pltpu.SemaphoreType.DMA((27,)), pltpu.SemaphoreType.DMA((2,))],
        compiler_params=pltpu.CompilerParams(vmem_limit_bytes=24 * 2**20),
        name="fdtd_steps",
    )(pos, flags, tables, *pieces)


def body(electric, magnetic, material, incoming, shift_flags, eps_table, sigma_table, kerr_table):
    count_z, count_y = lax.axis_size("gz"), lax.axis_size("gy")
    _, planes, rows, width = electric.shape
    hop = SHIFTS * SHIFT // planes
    assert hop * planes == SHIFTS * SHIFT and hop == 2 and planes == 2 * HALO
    assert rows == HALO and width == 2 * LANES and count_z % 2 == 0 and count_z >= 4
    gz, gy = lax.axis_index("gz"), lax.axis_index("gy")
    odd = gz % 2 == 1

    ids = material.astype(jnp.float32)
    fresh = incoming.astype(jnp.float32)

    moved_e = neighbour(electric, "gz", -hop)
    moved_hm = neighbour(jnp.concatenate([magnetic, ids[None]], 0), "gz", -hop)
    fresh_at = jnp.clip(gz - (count_z - hop), 0, hop - 1) * planes
    fresh_ids = lax.dynamic_slice_in_dim(fresh, fresh_at, planes, 0)
    moved_hm = jnp.concatenate(
        [moved_hm[:3], jnp.where(gz >= count_z - hop, fresh_ids, moved_hm[3])[None]], 0
    )

    def edge(field):
        return jnp.where(odd, field[:, HALO:], jnp.where(gz == 0, 0.0, field[:, :HALO]))

    edge_ids = jnp.where(odd, ids[HALO:], jnp.where(gz == 0, fresh[:HALO], ids[:HALO]))
    outer = jnp.concatenate([edge(electric), edge(magnetic), edge_ids[None]], 0)
    o_up, o_dn = neighbour(outer, "gy", -1), neighbour(outer, "gy", 1)
    o_all = outer_halo(jnp.stack([o_dn, outer, o_up]))

    def inner(field):
        return swap_cores(jnp.where(odd, field[:, :HALO], field[:, HALO:]))

    def around(field):
        up, dn = neighbour(field, "gy", -1), neighbour(field, "gy", 1)
        return [dn, field, up], [inner(dn), inner(field), inner(up)]

    e_main, e_inner = around(moved_e)
    h_main, h_inner = around(moved_hm)

    tables = jnp.stack(
        [4.0 * eps_table - 2.0 * sigma_table, 4.0 * eps_table + 2.0 * sigma_table, 4.0 * kerr_table]
    )
    tables = jnp.broadcast_to(jnp.pad(tables, ((0, 0), (0, LANES - MAT)))[:, None, :], (3, 8, LANES))
    pos = jnp.stack([gz, gy, count_y - 1, count_z * planes]).astype(jnp.int32)
    pieces = e_main + h_main + e_inner + h_inner + [o_all[0], o_all[1], o_all[2]]
    return run_steps(pos, shift_flags, tables, pieces, planes, rows, width)


def solution(mesh):
    field = P(None, "gz", "gy", None)
    return jax.shard_map(
        body,
        mesh=mesh,
        in_specs=(field, field, P("gz", "gy", None), P(None, "gy", None), P(), P(), P(), P()),
        out_specs=(field, field),
        check_vma=False,
    )
```

```python
import functools

import jax
import jax.numpy as jnp
from jax import lax
from jax.experimental import pallas as pl
from jax.experimental.pallas import tpu as pltpu
from jax.sharding import PartitionSpec as P

STEPS = 8
SHIFTS = 4
SHIFT = 8
HALO = STEPS
MAT = 16
LANES = 128
TILE = 8
TILES = 3
PAD = 8
GROUP = 8
HALVES = (slice(0, LANES), slice(LANES, 2 * LANES))


def e_at(t, off=0):
    return slice(TILE * t + off, TILE * t + off + TILE)


def h_at(t, off=0):
    return slice(TILE * (t + 1) + off, TILE * (t + 1) + off + TILE)


def assemble(planes, odd, first, outer_first, own, other, near, far, outer, store):
    inner_at = (1 - odd) * (planes + HALO)
    outer_at = odd * (planes + HALO)
    near_row = odd * (2 * TILE)
    far_row = (2 - 2 * odd) * TILE

    def run(count, pick, at, row):
        def one(p, carry):
            for c in range(3):
                for i, x in enumerate(HALVES):
                    store(c, at + p, i, row, pick(c, p, x))
            return carry

        lax.fori_loop(0, count, one, 0, unroll=4)

    skip = odd * HALO
    run(planes, lambda c, p, x: own[first + c, p, :, x], HALO, TILE)
    run(HALO, lambda c, p, x: other[first + c, skip + p, :, x], inner_at, TILE)
    run(planes, lambda c, p, x: near[0, first + c, p, :, x], HALO, near_row)
    run(HALO, lambda c, p, x: near[1, first + c, skip + p, :, x], inner_at, near_row)
    run(planes, lambda c, p, x: far[first + c, p, :, x], HALO, far_row)
    run(HALO, lambda c, p, x: far[first + c, planes + p, :, x], inner_at, far_row)
    for t in range(TILES):
        run(HALO, lambda c, p, x: outer[t, outer_first + c, p, :, x], outer_at, TILE * t)


def prepare_kernel(planes, pos, tables, own, other, near, far, outer, E, A, B, K, ids):
    odd = lax.rem(pos[0], 2)

    def store(c, p, i, row, value):
        E[c, p, i, pl.ds(pl.multiple_of(row, TILE), TILE), :] = value

    assemble(planes, odd, 0, 0, own, other, near, far, outer, store)

    def store_id(c, p, i, row, value):
        if c == 0:
            ids[p, i, pl.ds(pl.multiple_of(row, TILE), TILE), :] = value

    assemble(planes, odd, 3, 6, IdsView(own), IdsView(other), IdsView(near), IdsView(far), IdsView(outer), store_id)

    def look_up(p, carry):
        for t in range(TILES):
            for i in range(2):
                index = ids[p, i, e_at(t), :].astype(jnp.int32)
                for k, out in enumerate((A, B, K)):
                    out[p, i, e_at(t), :] = jnp.take_along_axis(tables[k], index, axis=1)
        return carry

    lax.fori_loop(0, planes + 2 * HALO, look_up, 0, unroll=4)


class IdsView:
    def __init__(self, ref):
        self.ref = ref
        self.at = ref.shape[-4] - 1

    def __getitem__(self, key):
        key = list(key)
        key[-4] = self.at
        return self.ref[tuple(key)]


def step_kernel(
    planes, pos, flags, E0, A, B, K, own, other, near, far, outer,
    e_out, h_out, E1, E2, H1, H2, e_stage, h_stage, out_sems,
):
    gz, gy, last_y, top_z = pos[0], pos[1], pos[2], pos[3]
    wide = planes + 2 * HALO
    odd = lax.rem(gz, 2)
    shape = (TILE, LANES)
    lane = lax.broadcasted_iota(jnp.int32, shape, 1)
    sub = lax.broadcasted_iota(jnp.int32, shape, 0)
    lane_first, lane_last = lane == 0, lane == LANES - 1
    below = jnp.where((gy == 0) & (sub == 0), 0.0, 1.0).astype(jnp.float32)
    above = jnp.where((gy == last_y) & (sub == TILE - 1), 0.0, 1.0).astype(jnp.float32)

    def store(c, p, i, row, value):
        H1[c, p, i, pl.ds(pl.multiple_of(row + TILE, TILE), TILE), :] = 2.0 * value

    assemble(planes, odd, 0, 3, own, other, near, far, outer, store)

    def x_next(v):
        r = [pltpu.roll(a, LANES - 1, 1) for a in v]
        return [jnp.where(lane_last, r[1], r[0]), jnp.where(lane_last, 0.0, r[1])]

    def x_prev(v):
        r = [pltpu.roll(a, 1, 1) for a in v]
        return [jnp.where(lane_first, 0.0, r[0]), jnp.where(lane_first, r[0], r[1])]

    def magnetic_plane(E, Hi, Ho, p, last):
        for t in range(TILES - 1 if last else TILES):
            def get(c, dp=0, off=0):
                return [E[c, p + dp, i, e_at(t, off), :] for i in range(2)]

            ex, ey, ez = get(0), get(1), get(2)
            ez_x, ey_x = x_next(ez), x_next(ey)
            ez_y, ex_y = get(2, 0, 1), get(0, 0, 1)
            if t == 1:
                ez_y, ex_y = [a * above for a in ez_y], [a * above for a in ex_y]
            ey_z, ex_z = get(1, 1), get(0, 1)
            for i in range(2):
                old = [Hi[c, p, i, h_at(t), :] for c in range(3)]
                Ho[0, p, i, h_at(t), :] = old[0] - ((ez_y[i] - ez[i]) - (ey_z[i] - ey[i]))
                Ho[1, p, i, h_at(t), :] = old[1] - ((ex_z[i] - ex[i]) - (ez_x[i] - ez[i]))
                Ho[2, p, i, h_at(t), :] = old[2] - ((ey_x[i] - ey[i]) - (ex_y[i] - ex[i]))

    def electric_plane(H, Ei, Eo, p, last):
        for t in [1] if last else range(TILES):
            def get(c, dp=0, off=0):
                return [H[c, p + dp, i, h_at(t, off), :] for i in range(2)]

            hx, hy, hz = get(0), get(1), get(2)
            hz_x, hy_x = x_prev(hz), x_prev(hy)
            hz_y, hx_y = get(2, 0, -1), get(0, 0, -1)
            if t == 1:
                hz_y, hx_y = [a * below for a in hz_y], [a * below for a in hx_y]
            hy_z, hx_z = get(1, -1), get(0, -1)
            for i in range(2):
                ex, ey, ez = [Ei[c, p, i, e_at(t), :] for c in range(3)]
                cx = (hz[i] - hz_y[i]) - (hy[i] - hy_z[i])
                cy = (hx[i] - hx_z[i]) - (hz[i] - hz_x[i])
                cz = (hy[i] - hy_x[i]) - (hx[i] - hx_y[i])
                n = K[p, i, e_at(t), :] * (ex * ex + ey * ey + ez * ez)
                up = A[p, i, e_at(t), :] + n
                r = pltpu.reciprocal(B[p, i, e_at(t), :] + n, approx=True)
                for c, (e, curl) in enumerate(((ex, cx), (ey, cy), (ez, cz))):
                    if last:
                        Eo[c, p - HALO, :, HALVES[i]] = (up * e + curl) * r
                    else:
                        Eo[c, p, i, e_at(t), :] = (up * e + curl) * r

    def zero_plane(ref, p, count):
        @pl.when((p >= 0) & (p < count))
        def _():
            ref[:, p] = jnp.zeros((3,) + ref.shape[2:], jnp.float32)

    base = planes * gz + SHIFT * SHIFTS - HALO

    def grouped(plane, start, count):
        def one(g, carry):
            for j in range(GROUP):
                plane(start + g * GROUP + j)
            return carry

        lax.fori_loop(0, lax.div(count + GROUP - 1, GROUP), one, 0)

    h_copy = pltpu.make_async_copy(h_stage, h_out, out_sems.at[1])
    e_copy = pltpu.make_async_copy(e_stage, e_out, out_sems.at[0])

    def step(s, moved, Ei, Eo, Hi, Ho, last=False):
        moved = moved + flags[s - 1]
        grouped(lambda p: magnetic_plane(Ei, Hi, Ho, p, last), s - 1, wide + 1 - 2 * s)
        zero_plane(Ho, SHIFT * moved - 1 - base, wide)
        if last:
            def finish(p, carry):
                for c in range(3):
                    for i in range(2):
                        h_stage[c, p, :, HALVES[i]] = 0.5 * Ho[c, HALO + p, i, h_at(1), :]
                return carry

            lax.fori_loop(0, planes, finish, 0, unroll=4)
            h_copy.start()
        grouped(lambda p: electric_plane(Ho, Ei, Eo, p, last), s, wide - 2 * s)
        above_window = top_z + SHIFT * moved - base
        if last:
            zero_plane(Eo, above_window - HALO, planes)
        else:
            zero_plane(Eo, above_window, wide)
        return moved

    moved = step(1, jnp.int32(0), E0, E1, H1, H2)

    def pair(k, moved):
        moved = step(2 * k, moved, E1, E2, H2, H1)
        return step(2 * k + 1, moved, E2, E1, H1, H2)

    moved = lax.fori_loop(1, STEPS // 2, pair, moved)
    step(STEPS, moved, E1, e_stage, H2, H1, last=True)
    e_copy.start()
    h_copy.wait()
    e_copy.wait()


SMEM, VMEM, ANY = [pl.BlockSpec(memory_space=m) for m in (pltpu.SMEM, pltpu.VMEM, pl.ANY)]


def prepare(pos, tables, pieces, planes):
    deep = planes + 2 * HALO + PAD
    coef = jax.ShapeDtypeStruct((deep, 2, TILES * TILE, LANES), jnp.float32)
    return pl.pallas_call(
        functools.partial(prepare_kernel, planes),
        out_shape=(jax.ShapeDtypeStruct((3, deep, 2, 4 * TILE, LANES), jnp.float32), coef, coef, coef),
        in_specs=[SMEM] + [VMEM] * (1 + len(pieces)),
        out_specs=(VMEM,) * 4,
        scratch_shapes=[pltpu.VMEM(coef.shape, jnp.float32)],
        compiler_params=pltpu.CompilerParams(vmem_limit_bytes=24 * 2**20),
        name="prepare",
    )(pos, tables, *pieces)


def run_steps(pos, flags, full, pieces, planes, rows, width):
    deep = planes + 2 * HALO + PAD
    field = jax.ShapeDtypeStruct((3, planes, rows, width), jnp.float32)
    work = pltpu.VMEM((3, deep, 2, 4 * TILE, LANES), jnp.float32)
    return pl.pallas_call(
        functools.partial(step_kernel, planes),
        out_shape=(field, field),
        in_specs=[SMEM, SMEM] + [VMEM] * (len(full) + len(pieces)),
        out_specs=(ANY,) * 2,
        scratch_shapes=[work] * 4
        + [pltpu.VMEM(field.shape, jnp.float32)] * 2
        + [pltpu.SemaphoreType.DMA((2,))],
        compiler_params=pltpu.CompilerParams(vmem_limit_bytes=32 * 2**20),
        name="fdtd_steps",
    )(pos, flags, *full, *pieces)


def down(value, hop, wrap=0):
    count = lax.axis_size("gz")
    pairs = [(s, s - hop) for s in range(hop, count)] + [(s, count + s - hop) for s in range(wrap)]
    return lax.ppermute(value, "gz", pairs)


def swap_cores(value):
    return lax.ppermute(value, "gz", [(s, s ^ 1) for s in range(lax.axis_size("gz"))])


def y_halo(value):
    nz, ny = lax.axis_size("gz"), lax.axis_size("gy")
    pairs = []
    for z in range(nz):
        hop = 1 - 2 * (z % 2)
        pairs += [(z * ny + y, z * ny + y + hop) for y in range(ny) if 0 <= y + hop < ny]
    return lax.ppermute(value, ("gz", "gy"), pairs)


def body(electric, magnetic, material, incoming, shift_flags, eps_table, sigma_table, kerr_table):
    count_z, count_y = lax.axis_size("gz"), lax.axis_size("gy")
    _, planes, rows, width = electric.shape
    hop = SHIFTS * SHIFT // planes
    assert hop * planes == SHIFTS * SHIFT and hop == 2 and planes == 2 * HALO
    assert rows == HALO and width == 2 * LANES and count_z % 2 == 0 and count_z >= 4
    gz, gy = lax.axis_index("gz"), lax.axis_index("gy")
    odd = gz % 2 == 1

    moved_e = down(jnp.concatenate([electric, material.astype(jnp.float32)[None]], 0), hop)
    moved_h = down(magnetic, hop)

    def edge(field):
        return jnp.where(odd, field[..., HALO:, :, :], field[..., :HALO, :, :])

    fields = jnp.concatenate([edge(electric), edge(magnetic)], 0)
    fresh = jnp.where(gz == 0, incoming[:HALO], edge(material)).astype(jnp.float32)
    mine = jnp.concatenate([jnp.where(gz == 0, 0.0, fields), fresh[None]], 0)
    theirs = swap_cores(mine)
    mine_y, theirs_y = y_halo(jnp.stack([mine, theirs]))
    part = HALO // 2
    crossed = down(
        jnp.where(
            odd,
            jnp.concatenate([theirs_y, theirs[:, part:]], 1),
            jnp.concatenate([mine_y, mine[:, :part]], 1),
        ),
        2 * hop,
        wrap=2,
    )
    given = swap_cores(jnp.where(odd, jnp.concatenate([mine_y, crossed[:, HALO:]], 1), crossed))
    outer = jnp.stack(
        [
            jnp.where(odd, given[:, :HALO], theirs_y),
            jnp.where(odd, jnp.concatenate([given[:, HALO:], crossed[:, HALO:]], 1), theirs),
            jnp.where(odd, crossed[:, :HALO], given[:, :HALO]),
        ]
    )

    def around(own):
        other = swap_cores(own)
        near = y_halo(jnp.stack([own, other]))
        edge_rows = jnp.where(odd, near[0, :, :HALO], near[0, :, HALO:])
        far = swap_cores(jnp.concatenate([near[1], edge_rows], 1))
        return [own, other, near, far]

    fresh_at = jnp.clip(gz - (count_z - hop), 0, hop - 1) * planes
    entering = lax.dynamic_slice_in_dim(incoming, fresh_at, planes, 0).astype(jnp.float32)
    ids = jnp.where(gz >= count_z - hop, entering, moved_e[3])
    e_pieces = around(jnp.concatenate([moved_e[:3], ids[None]], 0))
    h_pieces = around(moved_h)

    tables = jnp.stack(
        [4.0 * eps_table - 2.0 * sigma_table, 4.0 * eps_table + 2.0 * sigma_table, 4.0 * kerr_table]
    )
    tables = jnp.broadcast_to(jnp.pad(tables, ((0, 0), (0, LANES - MAT)))[:, None, :], (3, TILE, LANES))
    pos = jnp.stack([gz, gy, count_y - 1, count_z * planes]).astype(jnp.int32)
    full = prepare(pos, tables, e_pieces + [outer], planes)
    return run_steps(pos, shift_flags, full, h_pieces + [outer], planes, rows, width)


def solution(mesh):
    field = P(None, "gz", "gy", None)
    return jax.shard_map(
        body,
        mesh=mesh,
        in_specs=(field, field, P("gz", "gy", None), P(None, "gy", None), P(), P(), P(), P()),
        out_specs=(field, field),
        check_vma=False,
    )
```

```python
import functools

import jax
import jax.numpy as jnp
from jax import lax
from jax.experimental import pallas as pl
from jax.experimental.pallas import tpu as pltpu
from jax.sharding import PartitionSpec as P

STEPS = 8
SHIFTS = 4
SHIFT = 8
HALO = STEPS
MAT = 16
LANES = 128
TILE = 8
TILES = 3
PAD = 8
GROUP = 8
HALVES = (slice(0, LANES), slice(LANES, 2 * LANES))


def e_at(t, off=0):
    return slice(TILE * t + off, TILE * t + off + TILE)


def h_at(t, off=0):
    return slice(TILE * (t + 1) + off, TILE * (t + 1) + off + TILE)


def assemble(planes, odd, first, outer_first, pieces, store):
    pieces = [*pieces[:3], *[pieces[3].at[t] for t in range(TILES)], *[pieces[4].at[t] for t in range(TILES)]]
    inner_at = (1 - odd) * (planes + HALO)
    outer_at = odd * (planes + HALO)
    places = [(at, t * TILE) for at in (HALO, inner_at, outer_at) for t in range(TILES)]

    for k, (ref, (at, row)) in enumerate(zip(pieces, places)):
        start = outer_first if k >= 6 else first

        def one(p, carry, ref=ref, start=start, at=at, row=row):
            for c in range(3):
                for i, x in enumerate(HALVES):
                    store(c, at + p, i, row, ref, start, p, x)
            return carry

        lax.fori_loop(0, ref.shape[1], one, 0, unroll=4)


def start_kernel(planes, pos, electric, magnetic, material, incoming, edge, block, entering, ids, late, fresh, sems):
    gz, count_z = pos[0], pos[4]
    edge_at = lax.rem(gz, 2) * HALO
    late_at = jnp.clip(gz - count_z + 2, 0, 1) * planes
    near = pl.ds(edge_at, HALO)
    pairs = [(material, ids), (incoming.at[pl.ds(0, HALO)], fresh)]
    pairs += [(electric.at[c], block.at[c]) for c in range(3)]
    pairs += [(magnetic.at[c, near], edge.at[3 + c]) for c in range(3)]
    pairs += [(incoming.at[pl.ds(late_at, planes)], late)]
    copies = [pltpu.make_async_copy(src, dst, sems.at[i]) for i, (src, dst) in enumerate(pairs)]
    for one in copies:
        one.start()
    for one in copies:
        one.wait()
    block[3] = ids[...].astype(jnp.float32)
    entering[...] = late[...].astype(jnp.float32)
    for p in range(HALO):
        for c in range(3):
            edge[c, p] = block[c, edge_at + p]
        edge[6, p] = jnp.where(gz == 0, fresh[p], ids[edge_at + p]).astype(jnp.float32)

    @pl.when(gz == 0)
    def _():
        edge[0:6] = jnp.zeros((6,) + edge.shape[1:], jnp.float32)


def prepare_kernel(planes, pos, tables, *refs):
    pieces, (E, A, B, K, ids) = refs[:5], refs[5:]
    odd = lax.rem(pos[0], 2)

    def store(c, p, i, row, ref, start, q, x):
        at = pl.ds(row, TILE)
        E[c, p, i, at, :] = ref[start + c, q, :, x]
        if c == 0:
            ids[p, i, at, :] = ref[ref.shape[0] - 1, q, :, x]

    assemble(planes, odd, 0, 0, pieces, store)

    def look_up(p, carry):
        for t in range(TILES):
            for i in range(2):
                index = ids[p, i, e_at(t), :].astype(jnp.int32)
                for k, out in enumerate((A, B, K)):
                    out[p, i, e_at(t), :] = jnp.take_along_axis(tables[k], index, axis=1)
        return carry

    lax.fori_loop(0, planes + 2 * HALO, look_up, 0, unroll=4)


def step_kernel(
    planes, pos, flags, E0, A, B, K, *refs
):
    pieces, (e_out, h_out, E1, E2, H1, H2, e_stage, h_stage, out_sems) = refs[:5], refs[5:]
    gz, gy, last_y, top_z = pos[0], pos[1], pos[2], pos[3]
    wide = planes + 2 * HALO
    odd = lax.rem(gz, 2)
    shape = (TILE, LANES)
    lane = lax.broadcasted_iota(jnp.int32, shape, 1)
    sub = lax.broadcasted_iota(jnp.int32, shape, 0)
    lane_first, lane_last = lane == 0, lane == LANES - 1
    below = jnp.where((gy == 0) & (sub == 0), 0.0, 1.0).astype(jnp.float32)
    above = jnp.where((gy == last_y) & (sub == TILE - 1), 0.0, 1.0).astype(jnp.float32)

    def store(c, p, i, row, ref, start, q, x):
        H1[c, p, i, pl.ds(row + TILE, TILE), :] = 2.0 * ref[start + c, q, :, x]

    assemble(planes, odd, 0, 3, pieces, store)

    def x_next(v):
        r = [pltpu.roll(a, LANES - 1, 1) for a in v]
        return [jnp.where(lane_last, r[1], r[0]), jnp.where(lane_last, 0.0, r[1])]

    def x_prev(v):
        r = [pltpu.roll(a, 1, 1) for a in v]
        return [jnp.where(lane_first, 0.0, r[0]), jnp.where(lane_first, r[0], r[1])]

    def magnetic_plane(E, Hi, Ho, p, last):
        for t in range(TILES - 1 if last else TILES):
            def get(c, dp=0, off=0):
                return [E[c, p + dp, i, e_at(t, off), :] for i in range(2)]

            ex, ey, ez = get(0), get(1), get(2)
            ez_x, ey_x = x_next(ez), x_next(ey)
            ez_y, ex_y = get(2, 0, 1), get(0, 0, 1)
            if t == 1:
                ez_y, ex_y = [a * above for a in ez_y], [a * above for a in ex_y]
            ey_z, ex_z = get(1, 1), get(0, 1)
            for i in range(2):
                old = [Hi[c, p, i, h_at(t), :] for c in range(3)]
                Ho[0, p, i, h_at(t), :] = old[0] - ((ez_y[i] - ez[i]) - (ey_z[i] - ey[i]))
                Ho[1, p, i, h_at(t), :] = old[1] - ((ex_z[i] - ex[i]) - (ez_x[i] - ez[i]))
                Ho[2, p, i, h_at(t), :] = old[2] - ((ey_x[i] - ey[i]) - (ex_y[i] - ex[i]))

    def electric_plane(H, Ei, Eo, p, last):
        for t in [1] if last else range(TILES):
            def get(c, dp=0, off=0):
                return [H[c, p + dp, i, h_at(t, off), :] for i in range(2)]

            hx, hy, hz = get(0), get(1), get(2)
            hz_x, hy_x = x_prev(hz), x_prev(hy)
            hz_y, hx_y = get(2, 0, -1), get(0, 0, -1)
            if t == 1:
                hz_y, hx_y = [a * below for a in hz_y], [a * below for a in hx_y]
            hy_z, hx_z = get(1, -1), get(0, -1)
            for i in range(2):
                ex, ey, ez = [Ei[c, p, i, e_at(t), :] for c in range(3)]
                cx = (hz[i] - hz_y[i]) - (hy[i] - hy_z[i])
                cy = (hx[i] - hx_z[i]) - (hz[i] - hz_x[i])
                cz = (hy[i] - hy_x[i]) - (hx[i] - hx_y[i])
                n = K[p, i, e_at(t), :] * (ex * ex + ey * ey + ez * ez)
                up = A[p, i, e_at(t), :] + n
                r = pltpu.reciprocal(B[p, i, e_at(t), :] + n, approx=True)
                for c, (e, curl) in enumerate(((ex, cx), (ey, cy), (ez, cz))):
                    if last:
                        Eo[c, p - HALO, :, HALVES[i]] = (up * e + curl) * r
                    else:
                        Eo[c, p, i, e_at(t), :] = (up * e + curl) * r

    def zero_plane(ref, p, count):
        @pl.when((p >= 0) & (p < count))
        def _():
            ref[:, p] = jnp.zeros((3,) + ref.shape[2:], jnp.float32)

    base = planes * gz + SHIFT * SHIFTS - HALO

    def grouped(plane, start, count):
        def one(g, carry):
            for j in range(GROUP):
                plane(start + g * GROUP + j)
            return carry

        lax.fori_loop(0, lax.div(count + GROUP - 1, GROUP), one, 0)

    h_copy = pltpu.make_async_copy(h_stage, h_out, out_sems.at[1])
    e_copy = pltpu.make_async_copy(e_stage, e_out, out_sems.at[0])

    def step(s, moved, Ei, Eo, Hi, Ho, last=False):
        moved = moved + flags[s - 1]
        grouped(lambda p: magnetic_plane(Ei, Hi, Ho, p, last), s - 1, wide + 1 - 2 * s)
        zero_plane(Ho, SHIFT * moved - 1 - base, wide)
        if last:
            def finish(p, carry):
                for c in range(3):
                    for i in range(2):
                        h_stage[c, p, :, HALVES[i]] = 0.5 * Ho[c, HALO + p, i, h_at(1), :]
                return carry

            lax.fori_loop(0, planes, finish, 0, unroll=4)
            h_copy.start()
        grouped(lambda p: electric_plane(Ho, Ei, Eo, p, last), s, wide - 2 * s)
        above_window = top_z + SHIFT * moved - base
        if last:
            zero_plane(Eo, above_window - HALO, planes)
        else:
            zero_plane(Eo, above_window, wide)
        return moved

    moved = step(1, jnp.int32(0), E0, E1, H1, H2)

    def pair(k, moved):
        moved = step(2 * k, moved, E1, E2, H2, H1)
        return step(2 * k + 1, moved, E2, E1, H1, H2)

    moved = lax.fori_loop(1, STEPS // 2, pair, moved)
    step(STEPS, moved, E1, e_stage, H2, H1, last=True)
    e_copy.start()
    h_copy.wait()
    e_copy.wait()


SMEM, VMEM, ANY = [pl.BlockSpec(memory_space=m) for m in (pltpu.SMEM, pltpu.VMEM, pl.ANY)]


def start(pos, electric, magnetic, material, incoming, planes, rows, width):
    def shape(*lead):
        return jax.ShapeDtypeStruct(lead + (rows, width), jnp.float32)

    def whole(count):
        return pltpu.VMEM((count, rows, width), jnp.int32)

    return pl.pallas_call(
        functools.partial(start_kernel, planes),
        out_shape=(shape(7, HALO), shape(4, planes), shape(planes)),
        in_specs=[SMEM] + [ANY] * 4,
        out_specs=(VMEM,) * 3,
        scratch_shapes=[whole(planes), whole(planes), whole(HALO), pltpu.SemaphoreType.DMA((9,))],
        compiler_params=pltpu.CompilerParams(vmem_limit_bytes=60 * 2**20),
        name="start",
    )(pos, electric, magnetic, material, incoming)


def prepare(pos, tables, pieces, planes):
    deep = planes + 2 * HALO + PAD
    coef = jax.ShapeDtypeStruct((deep, 2, TILES * TILE, LANES), jnp.float32)
    return pl.pallas_call(
        functools.partial(prepare_kernel, planes),
        out_shape=(jax.ShapeDtypeStruct((3, deep, 2, 4 * TILE, LANES), jnp.float32), coef, coef, coef),
        in_specs=[SMEM] + [VMEM] * (1 + len(pieces)),
        out_specs=(VMEM,) * 4,
        scratch_shapes=[pltpu.VMEM(coef.shape, jnp.float32)],
        compiler_params=pltpu.CompilerParams(vmem_limit_bytes=4 * 2**20),
        cost_estimate=pl.CostEstimate(flops=0, bytes_accessed=32 * 2**20, transcendentals=0),
        name="prepare",
    )(pos, tables, *pieces)


def run_steps(pos, flags, full, pieces, planes, rows, width):
    deep = planes + 2 * HALO + PAD
    field = jax.ShapeDtypeStruct((3, planes, rows, width), jnp.float32)
    work = pltpu.VMEM((3, deep, 2, 4 * TILE, LANES), jnp.float32)
    return pl.pallas_call(
        functools.partial(step_kernel, planes),
        out_shape=(field, field),
        in_specs=[SMEM, SMEM] + [VMEM] * (len(full) + len(pieces)),
        out_specs=(ANY,) * 2,
        scratch_shapes=[work] * 4
        + [pltpu.VMEM(field.shape, jnp.float32)] * 2
        + [pltpu.SemaphoreType.DMA((2,))],
        compiler_params=pltpu.CompilerParams(vmem_limit_bytes=20 * 2**20),
        name="fdtd_steps",
    )(pos, flags, *full, *pieces)


def shift(value, axis, hop):
    count = lax.axis_size(axis)
    return lax.ppermute(value, axis, [(s, s + hop) for s in range(count) if 0 <= s + hop < count])


def outer_planes(value):
    count = lax.axis_size("gz")
    pairs = [(s, s - 1) for s in range(1, count, 2)] + [(s, s - 3) for s in range(4, count, 2)]
    return lax.ppermute(value, "gz", pairs + [(0, count - 3)])


def swap_cores(value):
    return lax.ppermute(value, "gz", [(s, s ^ 1) for s in range(lax.axis_size("gz"))])


def body(electric, magnetic, material, incoming, shift_flags, eps_table, sigma_table, kerr_table):
    count_z, count_y = lax.axis_size("gz"), lax.axis_size("gy")
    _, planes, rows, width = electric.shape
    hop = SHIFTS * SHIFT // planes
    assert hop * planes == SHIFTS * SHIFT and hop == 2 and planes == 2 * HALO
    assert rows == HALO and width == 2 * LANES and count_z % 2 == 0 and count_z >= 4
    gz, gy = lax.axis_index("gz"), lax.axis_index("gy")
    odd = gz % 2 == 1
    pos = jnp.stack([gz, gy, count_y - 1, count_z * planes, count_z]).astype(jnp.int32)

    edge, block, entering = start(pos, electric, magnetic, material, incoming, planes, rows, width)

    def spread(own):
        dn, up = shift(own, "gy", 1), shift(own, "gy", -1)
        return dn, up

    moved_e = shift(block, "gz", -hop)
    moved_h = shift(lax.optimization_barrier((magnetic, edge))[0], "gz", -hop)
    edge_dn, edge_up = spread(edge)
    outer = outer_planes(jnp.stack([edge_dn, edge, edge_up]))
    outer_pieces = [outer]

    def around(own):
        dn, up = spread(own)
        return [dn, own, up], jnp.stack([jnp.where(odd, field[:, :HALO], field[:, HALO:]) for field in (dn, own, up)])

    ids = jnp.where(gz >= count_z - hop, entering, moved_e[3])
    block = jnp.concatenate([moved_e[:3], ids[None]], 0)
    e_pieces, e_near = around(block)
    h_pieces, h_near = around(lax.optimization_barrier((moved_h, block, edge_dn, edge_up))[0])

    tables = jnp.stack(
        [4.0 * eps_table - 2.0 * sigma_table, 4.0 * eps_table + 2.0 * sigma_table, 4.0 * kerr_table]
    )
    tables = jnp.broadcast_to(jnp.pad(tables, ((0, 0), (0, LANES - MAT)))[:, None, :], (3, TILE, LANES))
    full = prepare(pos, tables, e_pieces + [swap_cores(e_near)] + outer_pieces, planes)
    h_near, *full = lax.optimization_barrier((h_near, *full))
    return run_steps(pos, shift_flags, full, h_pieces + [swap_cores(h_near)] + outer_pieces, planes, rows, width)


def solution(mesh):
    field = P(None, "gz", "gy", None)
    return jax.shard_map(
        body,
        mesh=mesh,
        in_specs=(field, field, P("gz", "gy", None), P(None, "gy", None), P(), P(), P(), P()),
        out_specs=(field, field),
        check_vma=False,
    )
```

```python
import functools

import jax
import jax.numpy as jnp
from jax import lax
from jax.experimental import pallas as pl
from jax.experimental.pallas import tpu as pltpu
from jax.sharding import PartitionSpec as P

STEPS = 8
SHIFTS = 4
SHIFT = 8
HALO = STEPS
MAT = 16
LANES = 128
TILE = 8
TILES = 3
PAD = 8
GROUP = 6
HALVES = (slice(0, LANES), slice(LANES, 2 * LANES))


def e_at(t, off=0):
    return slice(TILE * t + off, TILE * t + off + TILE)


def h_at(t, off=0):
    return slice(TILE * (t + 1) + off, TILE * (t + 1) + off + TILE)


def assemble(planes, odd, first, outer_first, pieces, store):
    pieces = [*pieces[:3], *[pieces[3].at[t] for t in range(TILES)], *[pieces[4].at[t] for t in range(TILES)]]
    inner_at = (1 - odd) * (planes + HALO)
    outer_at = odd * (planes + HALO)
    places = [(at, t * TILE) for at in (HALO, inner_at, outer_at) for t in range(TILES)]

    for k, (ref, (at, row)) in enumerate(zip(pieces, places)):
        start = outer_first if k >= 6 else first

        def one(p, carry, ref=ref, start=start, at=at, row=row):
            for c in range(3):
                for i, x in enumerate(HALVES):
                    store(c, at + p, i, row, ref, start, p, x)
            return carry

        lax.fori_loop(0, ref.shape[1], one, 0, unroll=4)


def start_kernel(planes, pos, electric, magnetic, material, incoming, edge, block, entering, ids, late, fresh, sems):
    gz, count_z = pos[0], pos[4]
    edge_at = lax.rem(gz, 2) * HALO
    late_at = jnp.clip(gz - count_z + 2, 0, 1) * planes
    near = pl.ds(edge_at, HALO)
    pairs = [(material, ids), (incoming.at[pl.ds(0, HALO)], fresh)]
    pairs += [(magnetic.at[c], block.at[c]) for c in range(3)]
    pairs += [(electric.at[c, near], edge.at[c]) for c in range(3)]
    pairs += [(incoming.at[pl.ds(late_at, planes)], late)]
    copies = [pltpu.make_async_copy(src, dst, sems.at[i]) for i, (src, dst) in enumerate(pairs)]
    for one in copies:
        one.start()
    for one in copies:
        one.wait()
    block[3] = ids[...].astype(jnp.float32)
    entering[...] = late[...].astype(jnp.float32)
    for p in range(HALO):
        for c in range(3):
            edge[3 + c, p] = block[c, edge_at + p]
        edge[6, p] = jnp.where(gz == 0, fresh[p], ids[edge_at + p]).astype(jnp.float32)

    @pl.when(gz == 0)
    def _():
        edge[0:6] = jnp.zeros((6,) + edge.shape[1:], jnp.float32)


def step_kernel(
    planes, pos, flags, tables, *refs
):
    e_pieces, h_pieces, outer, refs = refs[:4], refs[4:8], refs[8:9], refs[9:]
    e_out, h_out, E1, E2, H1, H2, A, B, K, ids, e_stage, h_stage, out_sems = refs
    gz, gy, last_y, top_z = pos[0], pos[1], pos[2], pos[3]
    wide = planes + 2 * HALO
    odd = lax.rem(gz, 2)
    shape = (TILE, LANES)
    lane = lax.broadcasted_iota(jnp.int32, shape, 1)
    sub = lax.broadcasted_iota(jnp.int32, shape, 0)
    lane_first, lane_last = lane == 0, lane == LANES - 1
    below = jnp.where((gy == 0) & (sub == 0), 0.0, 1.0).astype(jnp.float32)
    above = jnp.where((gy == last_y) & (sub == TILE - 1), 0.0, 1.0).astype(jnp.float32)

    def store_e(c, p, i, row, ref, start, q, x):
        at = pl.ds(row, TILE)
        E2[c, p, i, at, :] = ref[start + c, q, :, x]

    def store_h(c, p, i, row, ref, start, q, x):
        H1[c, p, i, pl.ds(row + TILE, TILE), :] = 2.0 * ref[start + c, q, :, x]
        if c == 0:
            ids[p, i, pl.ds(row, TILE), :] = ref[ref.shape[0] - 1, q, :, x]

    def look_up(p, carry):
        for t in range(TILES):
            for i in range(2):
                index = ids[p, i, e_at(t), :].astype(jnp.int32)
                for k, out in enumerate((A, B, K)):
                    out[p, i, e_at(t), :] = jnp.take_along_axis(tables[k], index, axis=1)
        return carry

    assemble(planes, odd, 0, 0, e_pieces + outer, store_e)
    assemble(planes, odd, 0, 3, h_pieces + outer, store_h)
    lax.fori_loop(0, wide, look_up, 0, unroll=8)

    def x_next(v):
        r = [pltpu.roll(a, LANES - 1, 1) for a in v]
        return [jnp.where(lane_last, r[1], r[0]), jnp.where(lane_last, 0.0, r[1])]

    def x_prev(v):
        r = [pltpu.roll(a, 1, 1) for a in v]
        return [jnp.where(lane_first, 0.0, r[0]), jnp.where(lane_first, r[0], r[1])]

    def magnetic_plane(E, Hi, Ho, p, last):
        for t in range(TILES - 1 if last else TILES):
            def get(c, dp=0, off=0):
                return [E[c, p + dp, i, e_at(t, off), :] for i in range(2)]

            ex, ey, ez = get(0), get(1), get(2)
            ez_x, ey_x = x_next(ez), x_next(ey)
            ez_y, ex_y = get(2, 0, 1), get(0, 0, 1)
            if t == 1:
                ez_y, ex_y = [a * above for a in ez_y], [a * above for a in ex_y]
            ey_z, ex_z = get(1, 1), get(0, 1)
            for i in range(2):
                old = [Hi[c, p, i, h_at(t), :] for c in range(3)]
                Ho[0, p, i, h_at(t), :] = old[0] - ((ez_y[i] - ez[i]) - (ey_z[i] - ey[i]))
                Ho[1, p, i, h_at(t), :] = old[1] - ((ex_z[i] - ex[i]) - (ez_x[i] - ez[i]))
                Ho[2, p, i, h_at(t), :] = old[2] - ((ey_x[i] - ey[i]) - (ex_y[i] - ex[i]))

    def electric_plane(H, Ei, Eo, p, last):
        for t in [1] if last else range(TILES):
            def get(c, dp=0, off=0):
                return [H[c, p + dp, i, h_at(t, off), :] for i in range(2)]

            hx, hy, hz = get(0), get(1), get(2)
            hz_x, hy_x = x_prev(hz), x_prev(hy)
            hz_y, hx_y = get(2, 0, -1), get(0, 0, -1)
            if t == 1:
                hz_y, hx_y = [a * below for a in hz_y], [a * below for a in hx_y]
            hy_z, hx_z = get(1, -1), get(0, -1)
            for i in range(2):
                ex, ey, ez = [Ei[c, p, i, e_at(t), :] for c in range(3)]
                cx = (hz[i] - hz_y[i]) - (hy[i] - hy_z[i])
                cy = (hx[i] - hx_z[i]) - (hz[i] - hz_x[i])
                cz = (hy[i] - hy_x[i]) - (hx[i] - hx_y[i])
                n = K[p, i, e_at(t), :] * (ex * ex + ey * ey + ez * ez)
                up = A[p, i, e_at(t), :] + n
                r = pltpu.reciprocal(B[p, i, e_at(t), :] + n, approx=True)
                for c, (e, curl) in enumerate(((ex, cx), (ey, cy), (ez, cz))):
                    if last:
                        Eo[c, p - HALO, :, HALVES[i]] = (up * e + curl) * r
                    else:
                        Eo[c, p, i, e_at(t), :] = (up * e + curl) * r

    def zero_plane(ref, p, count):
        @pl.when((p >= 0) & (p < count))
        def _():
            ref[:, p] = jnp.zeros((3,) + ref.shape[2:], jnp.float32)

    base = planes * gz + SHIFT * SHIFTS - HALO

    h_copy = pltpu.make_async_copy(h_stage, h_out, out_sems.at[1])
    e_copy = pltpu.make_async_copy(e_stage.at[:, pl.ds(0, planes)], e_out, out_sems.at[0])

    def step(s, moved, Ei, Eo, Hi, Ho, last=False):
        moved = moved + flags[s - 1]
        below_window = SHIFT * moved - 1 - base
        above_window = top_z + SHIFT * moved - base
        groups = lax.div(wide - 2 * s + GROUP - 1, GROUP)

        def close(start, count):
            @pl.when((below_window >= start) & (below_window < start + count))
            def _():
                Ho[:, below_window] = jnp.zeros((3,) + Ho.shape[2:], jnp.float32)

        def one(g, carry):
            start = s + g * GROUP
            for j in range(GROUP):
                electric_plane(Ho, Ei, Eo, start + j, last)
                magnetic_plane(Ei, Hi, Ho, start + GROUP + j, last)
            close(start + GROUP, GROUP)
            return carry

        for j in range(GROUP + 1):
            magnetic_plane(Ei, Hi, Ho, s - 1 + j, last)
        close(s - 1, GROUP + 1)
        lax.fori_loop(0, groups - 1, one, 0)
        if last:
            def finish(p, carry):
                for c in range(3):
                    for i in range(2):
                        h_stage[c, p, :, HALVES[i]] = 0.5 * Ho[c, HALO + p, i, h_at(1), :]
                return carry

            lax.fori_loop(0, planes, finish, 0, unroll=4)
            h_copy.start()
        for j in range(GROUP):
            electric_plane(Ho, Ei, Eo, s + (groups - 1) * GROUP + j, last)
        if last:
            zero_plane(Eo, above_window - HALO, planes)
        else:
            zero_plane(Eo, above_window, wide)
        return moved

    moved = step(1, jnp.int32(0), E2, E1, H1, H2)

    def pair(k, moved):
        moved = step(2 * k, moved, E1, E2, H2, H1)
        return step(2 * k + 1, moved, E2, E1, H1, H2)

    moved = lax.fori_loop(1, STEPS // 2, pair, moved)
    step(STEPS, moved, E1, e_stage, H2, H1, last=True)
    e_copy.start()
    h_copy.wait()
    e_copy.wait()


SMEM, VMEM, ANY = [pl.BlockSpec(memory_space=m) for m in (pltpu.SMEM, pltpu.VMEM, pl.ANY)]


def start(pos, electric, magnetic, material, incoming, planes, rows, width):
    def shape(*lead):
        return jax.ShapeDtypeStruct(lead + (rows, width), jnp.float32)

    def whole(count):
        return pltpu.VMEM((count, rows, width), jnp.int32)

    return pl.pallas_call(
        functools.partial(start_kernel, planes),
        out_shape=(shape(7, HALO), shape(4, planes), shape(planes)),
        in_specs=[SMEM] + [ANY] * 4,
        out_specs=(VMEM,) * 3,
        scratch_shapes=[whole(planes), whole(planes), whole(HALO), pltpu.SemaphoreType.DMA((9,))],
        compiler_params=pltpu.CompilerParams(vmem_limit_bytes=60 * 2**20),
        name="start",
    )(pos, electric, magnetic, material, incoming)


def run_steps(pos, flags, tables, pieces, planes, rows, width):
    deep = planes + 2 * HALO + PAD
    field = jax.ShapeDtypeStruct((3, planes, rows, width), jnp.float32)

    def vmem(*shape):
        return pltpu.VMEM(shape, jnp.float32)

    return pl.pallas_call(
        functools.partial(step_kernel, planes),
        out_shape=(field, field),
        in_specs=[SMEM, SMEM] + [VMEM] * (1 + len(pieces)),
        out_specs=(ANY,) * 2,
        scratch_shapes=[vmem(3, deep, 2, 4 * TILE, LANES)] * 4
        + [vmem(deep, 2, TILES * TILE, LANES)] * 4
        + [vmem(3, planes + GROUP, rows, width), vmem(*field.shape)]
        + [pltpu.SemaphoreType.DMA((2,))],
        compiler_params=pltpu.CompilerParams(vmem_limit_bytes=28 * 2**20),
        name="fdtd_steps",
    )(pos, flags, tables, *pieces)


def shift(value, axis, hop):
    count = lax.axis_size(axis)
    return lax.ppermute(value, axis, [(s, s + hop) for s in range(count) if 0 <= s + hop < count])


def outer_planes(value):
    count = lax.axis_size("gz")
    pairs = [(s, s - 1) for s in range(1, count, 2)] + [(s, s - 3) for s in range(4, count, 2)]
    return lax.ppermute(value, "gz", pairs + [(0, count - 3)])


def swap_cores(value):
    return lax.ppermute(value, "gz", [(s, s ^ 1) for s in range(lax.axis_size("gz"))])


def body(electric, magnetic, material, incoming, shift_flags, eps_table, sigma_table, kerr_table):
    count_z, count_y = lax.axis_size("gz"), lax.axis_size("gy")
    _, planes, rows, width = electric.shape
    hop = SHIFTS * SHIFT // planes
    assert hop * planes == SHIFTS * SHIFT and hop == 2 and planes == 2 * HALO
    assert rows == HALO and width == 2 * LANES and count_z % 2 == 0 and count_z >= 4
    gz, gy = lax.axis_index("gz"), lax.axis_index("gy")
    odd = gz % 2 == 1
    pos = jnp.stack([gz, gy, count_y - 1, count_z * planes, count_z]).astype(jnp.int32)

    edge, block, entering = start(pos, electric, magnetic, material, incoming, planes, rows, width)

    def spread(own):
        dn, up = shift(own, "gy", 1), shift(own, "gy", -1)
        return dn, up

    moved_e, moved_h = shift(electric, "gz", -hop), shift(block, "gz", -hop)
    edge_dn, edge_up = spread(edge)
    outer = outer_planes(jnp.stack([edge_dn, edge, edge_up]))
    outer_pieces = [outer]

    def around(own):
        dn, up = spread(own)
        return [dn, own, up], jnp.stack([jnp.where(odd, field[:, :HALO], field[:, HALO:]) for field in (dn, own, up)])

    ids = jnp.where(gz >= count_z - hop, entering, moved_h[3])
    moved_h = jnp.concatenate([moved_h[:3], ids[None]], 0)
    e_pieces, e_near = around(moved_e)
    h_pieces, h_near = around(lax.optimization_barrier((moved_h, moved_e, edge_dn, edge_up))[0])

    tables = jnp.stack(
        [4.0 * eps_table - 2.0 * sigma_table, 4.0 * eps_table + 2.0 * sigma_table, 4.0 * kerr_table]
    )
    tables = jnp.broadcast_to(jnp.pad(tables, ((0, 0), (0, LANES - MAT)))[:, None, :], (3, TILE, LANES))
    e_near = swap_cores(e_near)
    h_near, e_near = lax.optimization_barrier((h_near, e_near))
    pieces = e_pieces + [e_near] + h_pieces + [swap_cores(h_near)] + outer_pieces
    return run_steps(pos, shift_flags, tables, pieces, planes, rows, width)


def solution(mesh):
    field = P(None, "gz", "gy", None)
    return jax.shard_map(
        body,
        mesh=mesh,
        in_specs=(field, field, P("gz", "gy", None), P(None, "gy", None), P(), P(), P(), P()),
        out_specs=(field, field),
        check_vma=False,
    )
```

```python
import functools

import jax
import jax.numpy as jnp
from jax import lax
from jax.experimental import pallas as pl
from jax.experimental.pallas import tpu as pltpu
from jax.sharding import PartitionSpec as P

STEPS = 8
SHIFTS = 4
SHIFT = 8
HALO = STEPS
MAT = 16
LANES = 128
TILE = 8
TILES = 3
PAD = 8
GROUP = 6
HALVES = (slice(0, LANES), slice(LANES, 2 * LANES))


def e_at(t, off=0):
    return slice(TILE * t + off, TILE * t + off + TILE)


def h_at(t, off=0):
    return slice(TILE * (t + 1) + off, TILE * (t + 1) + off + TILE)


def assemble(planes, odd, first, outer_first, pieces, store):
    *pieces, outer = pieces
    if len(pieces) == 5:
        beside = [pieces[3].at[0], pieces[3].at[1], pieces[4].at[0]]
    else:
        beside = [pieces[3].at[t] for t in range(TILES)]
    pieces = [*pieces[:3], *beside, *[outer.at[t] for t in range(TILES)]]
    inner_at = (1 - odd) * (planes + HALO)
    outer_at = odd * (planes + HALO)
    places = [(at, t * TILE) for at in (HALO, inner_at, outer_at) for t in range(TILES)]

    for k, (ref, (at, row)) in enumerate(zip(pieces, places)):
        start = outer_first if k >= 6 else first

        def one(p, carry, ref=ref, start=start, at=at, row=row):
            for c in range(3):
                for i, x in enumerate(HALVES):
                    store(c, at + p, i, row, ref, start, p, x)
            return carry

        lax.fori_loop(0, ref.shape[1], one, 0, unroll=4)


def start_kernel(planes, pos, electric, magnetic, material, incoming, edge, block, entering, ids, late, fresh, sems):
    gz, count_z = pos[0], pos[4]
    edge_at = lax.rem(gz, 2) * HALO
    late_at = jnp.clip(gz - count_z + 2, 0, 1) * planes
    near = pl.ds(edge_at, HALO)
    pairs = [(material, ids), (incoming.at[pl.ds(0, HALO)], fresh)]
    pairs += [(magnetic.at[c], block.at[c]) for c in range(3)]
    pairs += [(electric.at[c, near], edge.at[c]) for c in range(3)]
    pairs += [(incoming.at[pl.ds(late_at, planes)], late)]
    copies = [pltpu.make_async_copy(src, dst, sems.at[i]) for i, (src, dst) in enumerate(pairs)]
    for one in copies:
        one.start()
    for one in copies:
        one.wait()
    block[3] = ids[...].astype(jnp.float32)
    entering[...] = late[...].astype(jnp.float32)
    for p in range(HALO):
        for c in range(3):
            edge[3 + c, p] = block[c, edge_at + p]
        edge[6, p] = jnp.where(gz == 0, fresh[p], ids[edge_at + p]).astype(jnp.float32)

    @pl.when(gz == 0)
    def _():
        edge[0:6] = jnp.zeros((6,) + edge.shape[1:], jnp.float32)


def step_kernel(
    planes, pos, flags, tables, *refs
):
    e_pieces, h_pieces, outer, refs = refs[:4], refs[4:9], refs[9:10], refs[10:]
    e_out, h_out, E1, E2, H1, H2, A, B, K, ids, e_stage, h_stage, out_sems = refs
    gz, gy, last_y, top_z = pos[0], pos[1], pos[2], pos[3]
    wide = planes + 2 * HALO
    odd = lax.rem(gz, 2)
    shape = (TILE, LANES)
    lane = lax.broadcasted_iota(jnp.int32, shape, 1)
    sub = lax.broadcasted_iota(jnp.int32, shape, 0)
    lane_first, lane_last = lane == 0, lane == LANES - 1
    below = jnp.where((gy == 0) & (sub == 0), 0.0, 1.0).astype(jnp.float32)
    above = jnp.where((gy == last_y) & (sub == TILE - 1), 0.0, 1.0).astype(jnp.float32)

    def store_e(c, p, i, row, ref, start, q, x):
        at = pl.ds(row, TILE)
        E2[c, p, i, at, :] = ref[start + c, q, :, x]

    def store_h(c, p, i, row, ref, start, q, x):
        H1[c, p, i, pl.ds(row + TILE, TILE), :] = 2.0 * ref[start + c, q, :, x]
        if c == 0:
            ids[p, i, pl.ds(row, TILE), :] = ref[ref.shape[0] - 1, q, :, x]

    def look_up(p, carry):
        for t in range(TILES):
            for i in range(2):
                index = ids[p, i, e_at(t), :].astype(jnp.int32)
                for k, out in enumerate((A, B, K)):
                    out[p, i, e_at(t), :] = jnp.take_along_axis(tables[k], index, axis=1)
        return carry

    assemble(planes, odd, 0, 0, e_pieces + outer, store_e)
    assemble(planes, odd, 0, 3, h_pieces + outer, store_h)
    lax.fori_loop(0, wide, look_up, 0, unroll=8)

    def x_next(v):
        r = [pltpu.roll(a, LANES - 1, 1) for a in v]
        return [jnp.where(lane_last, r[1], r[0]), jnp.where(lane_last, 0.0, r[1])]

    def x_prev(v):
        r = [pltpu.roll(a, 1, 1) for a in v]
        return [jnp.where(lane_first, 0.0, r[0]), jnp.where(lane_first, r[0], r[1])]

    def magnetic_plane(E, Hi, Ho, p, last):
        for t in range(TILES - 1 if last else TILES):
            def get(c, dp=0, off=0):
                return [E[c, p + dp, i, e_at(t, off), :] for i in range(2)]

            ex, ey, ez = get(0), get(1), get(2)
            ez_x, ey_x = x_next(ez), x_next(ey)
            ez_y, ex_y = get(2, 0, 1), get(0, 0, 1)
            if t == 1:
                ez_y, ex_y = [a * above for a in ez_y], [a * above for a in ex_y]
            ey_z, ex_z = get(1, 1), get(0, 1)
            for i in range(2):
                old = [Hi[c, p, i, h_at(t), :] for c in range(3)]
                Ho[0, p, i, h_at(t), :] = old[0] - ((ez_y[i] - ez[i]) - (ey_z[i] - ey[i]))
                Ho[1, p, i, h_at(t), :] = old[1] - ((ex_z[i] - ex[i]) - (ez_x[i] - ez[i]))
                Ho[2, p, i, h_at(t), :] = old[2] - ((ey_x[i] - ey[i]) - (ex_y[i] - ex[i]))

    def electric_plane(H, Ei, Eo, p, last):
        for t in [1] if last else range(TILES):
            def get(c, dp=0, off=0):
                return [H[c, p + dp, i, h_at(t, off), :] for i in range(2)]

            hx, hy, hz = get(0), get(1), get(2)
            hz_x, hy_x = x_prev(hz), x_prev(hy)
            hz_y, hx_y = get(2, 0, -1), get(0, 0, -1)
            if t == 1:
                hz_y, hx_y = [a * below for a in hz_y], [a * below for a in hx_y]
            hy_z, hx_z = get(1, -1), get(0, -1)
            for i in range(2):
                ex, ey, ez = [Ei[c, p, i, e_at(t), :] for c in range(3)]
                cx = (hz[i] - hz_y[i]) - (hy[i] - hy_z[i])
                cy = (hx[i] - hx_z[i]) - (hz[i] - hz_x[i])
                cz = (hy[i] - hy_x[i]) - (hx[i] - hx_y[i])
                n = K[p, i, e_at(t), :] * (ex * ex + ey * ey + ez * ez)
                up = A[p, i, e_at(t), :] + n
                r = pltpu.reciprocal(B[p, i, e_at(t), :] + n, approx=True)
                for c, (e, curl) in enumerate(((ex, cx), (ey, cy), (ez, cz))):
                    if last:
                        Eo[c, p - HALO, :, HALVES[i]] = (up * e + curl) * r
                    else:
                        Eo[c, p, i, e_at(t), :] = (up * e + curl) * r

    def zero_plane(ref, p, count):
        @pl.when((p >= 0) & (p < count))
        def _():
            ref[:, p] = jnp.zeros((3,) + ref.shape[2:], jnp.float32)

    base = planes * gz + SHIFT * SHIFTS - HALO

    h_copy = pltpu.make_async_copy(h_stage, h_out, out_sems.at[1])
    e_copy = pltpu.make_async_copy(e_stage.at[:, pl.ds(0, planes)], e_out, out_sems.at[0])

    def step(s, moved, Ei, Eo, Hi, Ho, last=False):
        moved = moved + flags[s - 1]
        below_window = SHIFT * moved - 1 - base
        above_window = top_z + SHIFT * moved - base
        groups = lax.div(wide - 2 * s + GROUP - 1, GROUP)

        def close(start, count):
            @pl.when((below_window >= start) & (below_window < start + count))
            def _():
                Ho[:, below_window] = jnp.zeros((3,) + Ho.shape[2:], jnp.float32)

        def one(g, carry):
            start = s + g * GROUP
            for j in range(GROUP):
                electric_plane(Ho, Ei, Eo, start + j, last)
                magnetic_plane(Ei, Hi, Ho, start + GROUP + j, last)
            close(start + GROUP, GROUP)
            return carry

        for j in range(GROUP + 1):
            magnetic_plane(Ei, Hi, Ho, s - 1 + j, last)
        close(s - 1, GROUP + 1)
        lax.fori_loop(0, groups - 1, one, 0)
        if last:
            def finish(p, carry):
                for c in range(3):
                    for i in range(2):
                        h_stage[c, p, :, HALVES[i]] = 0.5 * Ho[c, HALO + p, i, h_at(1), :]
                return carry

            lax.fori_loop(0, planes, finish, 0, unroll=4)
            h_copy.start()
        for j in range(GROUP):
            electric_plane(Ho, Ei, Eo, s + (groups - 1) * GROUP + j, last)
        if last:
            zero_plane(Eo, above_window - HALO, planes)
        else:
            zero_plane(Eo, above_window, wide)
        return moved

    moved = step(1, jnp.int32(0), E2, E1, H1, H2)

    def pair(k, moved):
        moved = step(2 * k, moved, E1, E2, H2, H1)
        return step(2 * k + 1, moved, E2, E1, H1, H2)

    moved = lax.fori_loop(1, STEPS // 2, pair, moved)
    step(STEPS, moved, E1, e_stage, H2, H1, last=True)
    e_copy.start()
    h_copy.wait()
    e_copy.wait()


SMEM, VMEM, ANY = [pl.BlockSpec(memory_space=m) for m in (pltpu.SMEM, pltpu.VMEM, pl.ANY)]


def start(pos, electric, magnetic, material, incoming, planes, rows, width):
    def shape(*lead):
        return jax.ShapeDtypeStruct(lead + (rows, width), jnp.float32)

    def whole(count):
        return pltpu.VMEM((count, rows, width), jnp.int32)

    return pl.pallas_call(
        functools.partial(start_kernel, planes),
        out_shape=(shape(7, HALO), shape(4, planes), shape(planes)),
        in_specs=[SMEM] + [ANY] * 4,
        out_specs=(VMEM,) * 3,
        scratch_shapes=[whole(planes), whole(planes), whole(HALO), pltpu.SemaphoreType.DMA((9,))],
        compiler_params=pltpu.CompilerParams(vmem_limit_bytes=60 * 2**20),
        name="start",
    )(pos, electric, magnetic, material, incoming)


def run_steps(pos, flags, tables, pieces, planes, rows, width):
    deep = planes + 2 * HALO + PAD
    field = jax.ShapeDtypeStruct((3, planes, rows, width), jnp.float32)

    def vmem(*shape):
        return pltpu.VMEM(shape, jnp.float32)

    return pl.pallas_call(
        functools.partial(step_kernel, planes),
        out_shape=(field, field),
        in_specs=[SMEM, SMEM] + [VMEM] * (1 + len(pieces)),
        out_specs=(ANY,) * 2,
        scratch_shapes=[vmem(3, deep, 2, 4 * TILE, LANES)] * 4
        + [vmem(deep, 2, TILES * TILE, LANES)] * 4
        + [vmem(3, planes + GROUP, rows, width), vmem(*field.shape)]
        + [pltpu.SemaphoreType.DMA((2,))],
        compiler_params=pltpu.CompilerParams(vmem_limit_bytes=28 * 2**20),
        name="fdtd_steps",
    )(pos, flags, tables, *pieces)


def shift(value, axis, hop):
    count = lax.axis_size(axis)
    return lax.ppermute(value, axis, [(s, s + hop) for s in range(count) if 0 <= s + hop < count])


def outer_planes(value):
    count = lax.axis_size("gz")
    pairs = [(s, s - 1) for s in range(1, count, 2)] + [(s, s - 3) for s in range(4, count, 2)]
    return lax.ppermute(value, "gz", pairs + [(0, count - 3)])


def swap_cores(value):
    return lax.ppermute(value, "gz", [(s, s ^ 1) for s in range(lax.axis_size("gz"))])


def body(electric, magnetic, material, incoming, shift_flags, eps_table, sigma_table, kerr_table):
    count_z, count_y = lax.axis_size("gz"), lax.axis_size("gy")
    _, planes, rows, width = electric.shape
    hop = SHIFTS * SHIFT // planes
    assert hop * planes == SHIFTS * SHIFT and hop == 2 and planes == 2 * HALO
    assert rows == HALO and width == 2 * LANES and count_z % 2 == 0 and count_z >= 4
    gz, gy = lax.axis_index("gz"), lax.axis_index("gy")
    odd = gz % 2 == 1
    pos = jnp.stack([gz, gy, count_y - 1, count_z * planes, count_z]).astype(jnp.int32)

    edge, block, entering = start(pos, electric, magnetic, material, incoming, planes, rows, width)

    def spread(own):
        dn, up = shift(own, "gy", 1), shift(own, "gy", -1)
        return dn, up

    moved_e, moved_h = shift(electric, "gz", -hop), shift(block, "gz", -hop)
    edge_dn, edge_up = spread(edge)
    outer = outer_planes(jnp.stack([edge_dn, edge, edge_up]))
    outer_pieces = [outer]

    def around(own):
        dn, up = spread(own)
        near = [jnp.where(odd, field[:, :HALO], field[:, HALO:]) for field in (dn, own, up)]
        return [dn, own, up], near

    ids = jnp.where(gz >= count_z - hop, entering, moved_h[3])
    moved_h = jnp.concatenate([moved_h[:3], ids[None]], 0)
    e_pieces, e_near = around(moved_e)
    h_pieces, h_near = around(lax.optimization_barrier((moved_h, moved_e, edge_dn, edge_up))[0])

    tables = jnp.stack(
        [4.0 * eps_table - 2.0 * sigma_table, 4.0 * eps_table + 2.0 * sigma_table, 4.0 * kerr_table]
    )
    tables = jnp.broadcast_to(jnp.pad(tables, ((0, 0), (0, LANES - MAT)))[:, None, :], (3, TILE, LANES))
    e_near = swap_cores(jnp.stack(e_near))
    up, e_near = lax.optimization_barrier((h_near[2], e_near))
    h_near = [swap_cores(jnp.stack(h_near[:2])), swap_cores(up[None])]
    pieces = e_pieces + [e_near] + h_pieces + h_near + outer_pieces
    return run_steps(pos, shift_flags, tables, pieces, planes, rows, width)


def solution(mesh):
    field = P(None, "gz", "gy", None)
    return jax.shard_map(
        body,
        mesh=mesh,
        in_specs=(field, field, P("gz", "gy", None), P(None, "gy", None), P(), P(), P(), P()),
        out_specs=(field, field),
        check_vma=False,
    )
```
